32 devices in a mesh: parts: 2 (over y), dp: 4 (over z), tensor: 2 (over x), sub: 2 (over core).
Axes of the slice: x: 2, y: 2, z: 4, core: 2. Of those that a mesh axis runs over, the one named last changes fastest.
Arguments:
- layer_normed_input: bfloat16 [8192, 8192], P(('parts', 'dp'), ('tensor', 'sub')), parts along dimension 0, may hold values from -6 to 6
- value_gradient: bfloat16 [8192, 1024], P(('parts', 'dp'), ('tensor', 'sub')), parts along dimension 0, may hold values from -6 to 6
- value_matrix: bfloat16 [8192, 1024], P(None, ('tensor', 'sub')), may hold values from -0.1875 to 0.1875
- adapter_down_table: bfloat16 [8, 16, 8192], P(('parts', 'dp'), None, ('tensor', 'sub')), parts along dimension 0, may hold values from -0.0625 to 0.0625
- adapter_up_table: bfloat16 [8, 16, 1024], P(('parts', 'dp'), None, ('tensor', 'sub')), parts along dimension 0, may hold values from -0.1875 to 0.1875
- live_token_count: int32 [8], P('parts'), parts along dimension 0, may hold values from 1 to 1920, as said below
- block_customer: int32 [64], P(('parts', 'dp')), parts along dimension 0, may hold values from 0 to 3, as said below
- customer_slot: int32 [8], P('parts'), parts along dimension 0, may hold values from 0 to 3, as said below
- dropout_flags: int32 [4096], P(('parts', 'dp')), parts along dimension 0, may hold values from -2147483648 to 2147483646
Outputs:
- input_grad: bfloat16 [8192, 8192], P(('parts', 'dp'), ('tensor', 'sub')), parts along dimension 0
- down_grad: float32 [8, 16, 8192], P(('parts', 'dp'), None, ('tensor', 'sub')), parts along dimension 0
- up_grad: float32 [8, 16, 1024], P(('parts', 'dp'), None, ('tensor', 'sub')), parts along dimension 0
The draws below stay inside these ranges and needn't reach their ends.
There are 2 independent parts, one for each index of `parts`. The reference program is written for one: setup_inputs(seed, part) draws one part's arguments, and reference() takes and returns one part's arrays. A program takes and returns all parts, laid end to end along the dimension named above; an argument that names none is the same for every part. Nothing has to cross between parts.
Inputs may be any that keep to these rules, and one draw needn't show every extreme that they name: `live_token_count`: the blocks of one tenant are consecutive; a tenant with c live tokens has exactly ceil(c / 128) blocks, so each tenant has one or more. `block_customer`: blocks of one tenant are consecutive and every tenant has a block. Each slot once; the adapters and the gradients of tenant t sit in row customer_slot[t].
All inputs are finite; a program needn't handle non-finite values.
Results may differ from the reference program's by a relative error of at most 0.012.
Values may be sent and summed in bfloat16 or wider, within the bound.
A program may use at most 128 MiB of HBM per device.

```python
import jax
import jax.numpy as jnp
from jax import lax

MODEL_WIDTH = 8192
VALUE_WIDTH = 1024
ADAPTER_RANK = 16
BLOCK = 128
TOK_DEV = 1024
TOKENS = 4096
BLOCKS = 32
TENANT_TOTAL = 4
N_TENSOR = 2
N_SUB = 2


def tenant_layout(key):
    first, third = jax.random.split(key, 2)
    heavy_extra = 2 * (TOK_DEV // BLOCK - 1)
    order = jax.random.permutation(first, TENANT_TOTAL).astype(jnp.int32)
    heavy = (order < TENANT_TOTAL // 2).astype(jnp.int32)
    block_number = 1 + heavy_extra * heavy
    labels = jax.random.permutation(third, TENANT_TOTAL).astype(jnp.int32)
    ends = jnp.cumsum(block_number)
    position = jnp.sum((jnp.arange(BLOCKS, dtype=jnp.int32)[:, None] >= ends[None, :]).astype(jnp.int32), 1)
    return (block_number, labels, labels[position], order)


def draw_live_token_count(key, part):
    block_number, labels, tenants_of_blocks, order = tenant_layout(key)
    key = jax.random.fold_in(key, 5)
    tail = jax.random.randint(key, (TENANT_TOTAL,), 1, BLOCK + 1)
    tail = jnp.where(order == 0, BLOCK, tail)
    counted = BLOCK * (block_number - 1) + tail
    return jnp.zeros((TENANT_TOTAL,), jnp.int32).at[labels].set(counted.astype(jnp.int32))


def draw_block_customer(key, part):
    block_number, labels, tenants_of_blocks, order = tenant_layout(key)
    return tenants_of_blocks.astype(jnp.int32)


def draw_customer_slot(key, part):
    key = jax.random.fold_in(key, 11)
    return jax.random.permutation(key, TENANT_TOTAL).astype(jnp.int32)


def set_ends(entries, rng, low, largest):
    extent = entries.shape
    place = [jax.random.randint(jax.random.fold_in(rng, axis), (), 0, extent[axis]) for axis in range(len(extent))]
    entries = entries.at[tuple(place)].set(low)
    longest = extent.index(max(extent))
    place[longest] = (place[longest] + 1) % extent[longest]
    return entries.at[tuple(place)].set(largest)


def levels(stream_key, dims, cuts, least, largest):
    gain = 1.0
    for dim, parts in cuts:
        draws = jax.random.uniform(jax.random.fold_in(jax.random.fold_in(stream_key, 6), dim), (parts,), jnp.float32, least / len(cuts), largest / len(cuts))
        gain = gain * jnp.repeat(jnp.exp(draws), dims[dim] // parts).reshape((-1,) + (1,) * (len(dims) - 1 - dim))
    return gain


def noise(key, dims, spread, bound, cuts=(), held_as=jnp.bfloat16):
    level = levels(key, dims, cuts, -0.22, 0.18) if cuts else 1.0
    array = jax.random.normal(key, dims, jnp.float32) * spread * level
    return jnp.minimum(jnp.maximum(array, -bound), bound).astype(held_as)


def setup_inputs(seed: int = 0, part: int = 0) -> dict:
    keys = jax.random.split(jax.random.key(seed), 10)
    part_keys = jax.random.split(jax.random.fold_in(keys[9], part), 10)
    return {
        "layer_normed_input": noise(part_keys[0], (TOKENS, MODEL_WIDTH), 1.0, 6.0, ((0, 4), (1, 4))),
        "value_gradient": noise(part_keys[1], (TOKENS, VALUE_WIDTH), 1.0, 6.0, ((0, 4), (1, 4))),
        "value_matrix": noise(keys[2], (MODEL_WIDTH, VALUE_WIDTH), (MODEL_WIDTH // 8) ** -0.5, 0.1875, ((1, 4),)),
        "adapter_down_table": noise(part_keys[3], (TENANT_TOTAL, ADAPTER_RANK, MODEL_WIDTH), MODEL_WIDTH ** -0.5, 0.0625, ((0, 4), (2, 4))),
        "adapter_up_table": noise(part_keys[4], (TENANT_TOTAL, ADAPTER_RANK, VALUE_WIDTH), VALUE_WIDTH ** -0.5, 0.1875, ((0, 4), (2, 4))),
        "live_token_count": draw_live_token_count(jax.random.fold_in(jax.random.fold_in(keys[9], part), 71), part),
        "block_customer": draw_block_customer(jax.random.fold_in(jax.random.fold_in(keys[9], part), 71), part),
        "customer_slot": draw_customer_slot(jax.random.fold_in(jax.random.fold_in(keys[9], part), 71), part),
        "dropout_flags": set_ends(jax.random.randint(part_keys[8], (TOKENS // 2,), -2147483648, 2147483647), jax.random.fold_in(part_keys[8], 1), -2147483648, 2147483646).astype(jnp.int32),
    }


adapter_scale = 2.0


def unpack_drop(words):
    shifts = jnp.arange(32, dtype=jnp.int32)
    bits_all = jnp.bitwise_and(jnp.right_shift(words[:, None], shifts[None, :]), 1)
    return (2.0 * bits_all.astype(jnp.float32)).reshape(words.shape[0] * 2, ADAPTER_RANK)


def reference(layer_normed_input, value_gradient, value_matrix, adapter_down_table, adapter_up_table, live_token_count, block_customer, customer_slot, dropout_flags):
    tenant_ids = jnp.arange(TENANT_TOTAL, dtype=jnp.int32)
    onehot = (block_customer[:, None] == tenant_ids[None, :]).astype(jnp.int32)
    earlier = jnp.cumsum(onehot, 0) - onehot
    segment_index = jnp.sum(onehot * earlier, 1)
    tenant_count = jnp.sum(onehot * live_token_count[None, :], 1)
    live_rows = jnp.clip(tenant_count - BLOCK * segment_index, 0, BLOCK)
    keep_rows = (jnp.arange(BLOCK, dtype=jnp.int32)[None, :] < live_rows[:, None]).reshape(TOKENS)
    grad_kept = jnp.where(keep_rows[:, None], value_gradient, jnp.zeros_like(value_gradient))
    dropout_keep = unpack_drop(dropout_flags)
    slot_block = customer_slot[block_customer]
    groups = N_TENSOR * N_SUB
    group_width = VALUE_WIDTH // groups

    def block_terms(items):
        rows_in, row_gradient, row_dropout, adapter_slot_index = items
        down_matrix = adapter_down_table[adapter_slot_index]
        up_matrix = adapter_up_table[adapter_slot_index]
        rank_input = jnp.dot(rows_in, down_matrix.T, preferred_element_type=jnp.float32)
        rank_feature_gradient = jnp.dot(row_gradient, up_matrix.T, preferred_element_type=jnp.float32)
        rank_after_dropout = rank_input * row_dropout
        rank_gradient = adapter_scale * rank_feature_gradient * row_dropout
        block_up_matrix = adapter_scale * jnp.dot(rank_after_dropout.T, row_gradient.astype(jnp.float32), precision=lax.Precision.HIGHEST)
        down_block = jnp.dot(rank_gradient.T, rows_in.astype(jnp.float32), precision=lax.Precision.HIGHEST)
        base = jnp.zeros((BLOCK, MODEL_WIDTH), jnp.float32)
        for group_index in range(groups):
            lower = group_index * group_width
            partial_sum = jnp.dot(row_gradient[:, lower:lower + group_width], value_matrix[:, lower:lower + group_width].T, preferred_element_type=jnp.float32)
            base = base + lax.optimization_barrier(partial_sum.astype(jnp.bfloat16)).astype(jnp.float32)
        adapter_term = jnp.dot(rank_gradient, down_matrix.astype(jnp.float32), precision=lax.Precision.HIGHEST)
        return (base + adapter_term).astype(jnp.bfloat16), down_block, block_up_matrix

    input_blocks, down_blocks, up_blocks = lax.map(block_terms, (layer_normed_input.reshape(BLOCKS, BLOCK, MODEL_WIDTH), grad_kept.reshape(BLOCKS, BLOCK, VALUE_WIDTH), dropout_keep.reshape(BLOCKS, BLOCK, ADAPTER_RANK), slot_block))
    select = (slot_block[:, None] == tenant_ids[None, :]).astype(jnp.float32)
    slot_count = jnp.zeros((TENANT_TOTAL,), jnp.int32).at[customer_slot].set(live_token_count).astype(jnp.float32)
    down_grad = jnp.einsum("bs,brd->srd", select, down_blocks, precision=lax.Precision.HIGHEST) / slot_count[:, None, None]
    up_grad = jnp.einsum("bs,brd->srd", select, up_blocks, precision=lax.Precision.HIGHEST) / slot_count[:, None, None]
    return input_blocks.reshape(TOKENS, MODEL_WIDTH), down_grad, up_grad
```

```python
import functools

import jax
import jax.numpy as jnp
from jax import lax
from jax.experimental import pallas as pl
from jax.experimental.pallas import tpu as pltpu
from jax.sharding import PartitionSpec as P

RANK = 16
BLOCK = 128
SCALE = 2.0
CHUNKS = 2
MESH = pl.DeviceIdType.MESH
F32 = jnp.float32
BF16 = jnp.bfloat16


def dot_nt(a, b):
    return lax.dot_general(a, b, (((1,), (1,)), ((), ())), preferred_element_type=F32)


def exchange(
    sizes,
    x_hbm, dy_ref, w_hbm, down_ref, up_ref, drop_ref, meta_ref, info_ref,
    wfull, dyfull, downall, gexp, live_ref, sums_ref,
    x_ref, downs, ups, infos, part, ranks, outgoing, incoming,
    x_sem, own_sem, tab_send, tab_recv, rk_send, rk_recv, out_send, out_recv,
    wx_send, wx_recv, wz_send, wz_recv, wy_send, wy_recv, wc_send, wc_recv,
    dx_send, dx_recv, dc_send, dc_recv,
):
    n_dp, n_t, n_s = sizes
    a, d, t, s = (lax.axis_index(n) for n in ("parts", "dp", "tensor", "sub"))
    me = t * n_s + s
    rows, width = x_ref.shape
    vl = dy_ref.shape[1]
    rk = down_ref.shape[0]
    quarter = width // 4
    piece = quarter // CHUNKS
    odd = lax.rem(d, 2)
    z_peer = {"dp": d + 1 - 2 * odd}
    y_peer = {"parts": 1 - a}
    core_peer = {"sub": 1 - s}

    def ahead(dt, ds):
        return lax.rem(t + dt, n_t), lax.rem(s + ds, n_s)

    def behind(dt, ds):
        return lax.rem(t - dt + n_t, n_t), lax.rem(s - ds + n_s, n_s)

    group = [(dt, ds) for dt in range(n_t) for ds in range(n_s) if (dt, ds) != (0, 0)]
    cross = [(dt, ds) for dt, ds in group if dt]

    def remote(src, dst, send, recv, peer):
        return pltpu.make_async_remote_copy(
            src_ref=src, dst_ref=dst, send_sem=send, recv_sem=recv,
            device_id=peer, device_id_type=MESH,
        )

    barrier = pltpu.get_barrier_semaphore()
    for dt, ds in group:
        pt, ps = ahead(dt, ds)
        pl.semaphore_signal(barrier, inc=1, device_id={"tensor": pt, "sub": ps}, device_id_type=MESH)
    for off in range(1, n_dp):
        pl.semaphore_signal(barrier, inc=1, device_id={"dp": lax.rem(d + off, n_dp)}, device_id_type=MESH)
    pl.semaphore_signal(barrier, inc=1, device_id=y_peer, device_id_type=MESH)
    x_copy = pltpu.make_async_copy(x_hbm, x_ref, x_sem)
    x_copy.start()
    downs[d] = down_ref[...]
    ups[d] = up_ref[...]
    pl.semaphore_wait(barrier, len(group) + n_dp)

    sent = []

    def go(copy):
        copy.start()
        sent.append(copy)

    for off in range(1, n_dp):
        to = {"dp": lax.rem(d + off, n_dp)}
        go(remote(info_ref, infos.at[off], tab_send.at[0, off], tab_recv.at[0, off], to))
        go(remote(up_ref, ups.at[d], tab_send.at[1, off], tab_recv.at[1, off], to))
        go(remote(down_ref, downs.at[d], tab_send.at[2, off], tab_recv.at[2, off], to))

    def span(q, c):
        return pl.ds(pl.multiple_of(q * quarter + c * piece, 16), piece)

    q_own = 2 * a + odd
    q_z = 2 * a + 1 - odd
    q_y = 2 * (1 - a) + odd
    q_yz = 2 * (1 - a) + 1 - odd
    for c in range(CHUNKS):
        for dt, ds in cross:
            pt, ps = ahead(dt, ds)
            start = (pt * n_s + ps) * width + q_own * quarter + c * piece
            src = w_hbm.at[pl.ds(pl.multiple_of(start, 16), piece)]
            k = dt * n_s + ds
            go(remote(src, wfull.at[me, span(q_own, c)], wx_send.at[k, c], wx_recv.at[k, c],
                      {"tensor": pt, "sub": ps}))

    for dt in range(1, n_t):
        go(remote(dy_ref, dyfull.at[me], dx_send.at[dt], dx_recv.at[dt], {"tensor": lax.rem(t + dt, n_t)}))
    go(remote(dy_ref, dyfull.at[me], dc_send.at[0], dc_recv.at[0], core_peer))
    other_rows = pl.ds(pl.multiple_of((t * n_s + 1 - s) * width, 16), width)
    go(remote(w_hbm.at[other_rows], wfull.at[me], wc_send, wc_recv, core_peer))
    own_w = pltpu.make_async_copy(
        w_hbm.at[pl.ds(pl.multiple_of(me * width, 16), width)], wfull.at[me], own_sem.at[0])
    own_w.start()
    own_dy = pltpu.make_async_copy(dy_ref, dyfull.at[me], own_sem.at[1])
    own_dy.start()

    for off in range(1, n_dp):
        frm = lax.rem(d - off + n_dp, n_dp)
        here = {"dp": frm}
        remote(info_ref, infos.at[off], tab_send.at[0, off], tab_recv.at[0, off], here).wait_recv()
        remote(up_ref, ups.at[frm], tab_send.at[1, off], tab_recv.at[1, off], here).wait_recv()
        remote(down_ref, downs.at[frm], tab_send.at[2, off], tab_recv.at[2, off], here).wait_recv()
    x_copy.wait()
    slots = n_dp * rk // RANK
    slot_tok = meta_ref[0:1, :]
    own_slot = lax.broadcasted_iota(jnp.int32, (slots, RANK, rows), 0) == slot_tok[None]
    down_map = downs[...].reshape(n_dp * rk, width)
    up_map = ups[...].reshape(n_dp * rk, vl)
    downall[...] = down_map
    in_all = dot_nt(down_map, x_ref[...]).reshape(slots, RANK, rows)
    grad_all = dot_nt(up_map, dy_ref[...]).reshape(slots, RANK, rows)
    part[0:RANK, :] = jnp.sum(jnp.where(own_slot, in_all, 0.0), 0).astype(BF16)
    part[RANK:2 * RANK, :] = jnp.sum(jnp.where(own_slot, grad_all, 0.0), 0).astype(BF16)
    for dt, ds in group:
        pt, ps = ahead(dt, ds)
        k = dt * n_s + ds
        go(remote(part, ranks.at[me], rk_send.at[k], rk_recv.at[k], {"tensor": pt, "sub": ps}))
    ranks[me] = part[...]

    def forward(dt, ds, c):
        ft, fs = behind(dt, ds)
        g = ft * n_s + fs
        k = dt * n_s + ds
        mine = wfull.at[g, span(q_own, c)]
        remote(mine, mine, wx_send.at[k, c], wx_recv.at[k, c], {"tensor": ft, "sub": fs}).wait_recv()
        go(remote(mine, mine, wz_send.at[k, c], wz_recv.at[k, c], z_peer))
        go(remote(mine, mine, wy_send.at[0, k, c], wy_recv.at[0, k, c], y_peer))

    for c in range(CHUNKS):
        for dt, ds in cross:
            forward(dt, ds, c)

    lane = lax.broadcasted_iota(jnp.int32, (1, rows), 1)
    limit = meta_ref[1:2, :]
    tenant = meta_ref[2:3, :]
    following = jnp.concatenate([infos[n_dp - 1, 0:1, :]] * (rows // BLOCK), axis=1)
    last_block = lane >= rows - BLOCK
    goes_on = last_block & (following == tenant) & (jnp.zeros_like(lane) + d < n_dp - 1)
    limit = jnp.where(goes_on, BLOCK, limit)
    live = (lax.rem(lane, BLOCK) < limit).astype(F32)
    live_ref[...] = jnp.broadcast_to(live, live_ref.shape)

    for dt, ds in group:
        ft, fs = behind(dt, ds)
        k = dt * n_s + ds
        remote(part, ranks.at[ft * n_s + fs], rk_send.at[k], rk_recv.at[k],
               {"tensor": ft, "sub": fs}).wait_recv()
    total = jnp.sum(ranks[...].astype(F32), 0)
    keep = drop_ref[...] * (SCALE * live)
    dropped = total[0:RANK] * keep
    grad_rank = total[RANK:2 * RANK] * keep
    dropped_all = jnp.where(own_slot, dropped[None], 0.0).reshape(n_dp * rk, rows).astype(BF16)
    grad_all = jnp.where(own_slot, grad_rank[None], 0.0).reshape(n_dp * rk, rows).astype(BF16)
    gexp[...] = grad_all
    up_part = jnp.dot(dropped_all, dy_ref[...], preferred_element_type=F32)
    outgoing[:, :, width:] = up_part.reshape(n_dp, rk, vl).astype(BF16)
    down_part = jnp.dot(grad_all, x_ref[...], preferred_element_type=F32)
    outgoing[:, :, :width] = down_part.reshape(n_dp, rk, width).astype(BF16)
    for off in range(1, n_dp):
        to = lax.rem(d + off, n_dp)
        go(remote(outgoing.at[to], incoming.at[off], out_send.at[off], out_recv.at[off], {"dp": to}))
    incoming[0] = outgoing[d]

    for c in range(CHUNKS):
        for dt, ds in cross:
            ft, fs = behind(dt, ds)
            k = dt * n_s + ds
            got = wfull.at[ft * n_s + fs, span(q_z, c)]
            remote(got, got, wz_send.at[k, c], wz_recv.at[k, c], z_peer).wait_recv()
            go(remote(got, got, wy_send.at[1, k, c], wy_recv.at[1, k, c], y_peer))
    for dt in range(1, n_t):
        ft = lax.rem(t - dt + n_t, n_t)
        got = dyfull.at[ft * n_s + s]
        remote(got, got, dx_send.at[dt], dx_recv.at[dt], {"tensor": ft}).wait_recv()
        go(remote(got, got, dc_send.at[dt], dc_recv.at[dt], core_peer))

    for off in range(1, n_dp):
        remote(outgoing.at[d], incoming.at[off], out_send.at[off], out_recv.at[off],
               {"dp": lax.rem(d - off + n_dp, n_dp)}).wait_recv()
    sums_ref[...] = jnp.sum(incoming[...].astype(F32), 0)

    for c in range(CHUNKS):
        for dt, ds in cross:
            ft, fs = behind(dt, ds)
            g = ft * n_s + fs
            k = dt * n_s + ds
            for j, q in enumerate((q_y, q_yz)):
                got = wfull.at[g, span(q, c)]
                remote(got, got, wy_send.at[j, k, c], wy_recv.at[j, k, c], y_peer).wait_recv()
    for dt in range(n_t):
        got = dyfull.at[lax.rem(t - dt + n_t, n_t) * n_s + 1 - s]
        remote(got, got, dc_send.at[dt], dc_recv.at[dt], core_peer).wait_recv()
    got = wfull.at[t * n_s + 1 - s]
    remote(got, got, wc_send, wc_recv, core_peer).wait_recv()
    own_w.wait()
    own_dy.wait()
    for copy in sent:
        copy.wait_send()


def product(dy_ref, w_ref, down_ref, gexp_ref, live_ref, out_ref, kept, ranked):
    groups, rows, _ = dy_ref.shape

    @pl.when(pl.program_id(0) == 0)
    def _():
        eye = lax.broadcasted_iota(jnp.int32, (BLOCK, BLOCK), 0) == lax.broadcasted_iota(
            jnp.int32, (BLOCK, BLOCK), 1)
        for b in range(rows // BLOCK):
            at = slice(b * BLOCK, (b + 1) * BLOCK)
            column = jnp.sum(jnp.where(eye, live_ref[0:1, at], 0.0), 1, keepdims=True)
            for g in range(groups):
                kept[g, at, :] = jnp.where(column > 0, dy_ref[g, at, :].astype(F32), 0.0).astype(BF16)
        ranked[...] = gexp_ref[...].astype(F32).T.astype(BF16)

    total = jnp.dot(ranked[...], down_ref[...], preferred_element_type=F32)
    for g in range(groups):
        total += dot_nt(kept[g], w_ref[g])
    out_ref[...] = total.astype(BF16)


def body(x, dy, w, down_table, up_table, live_token_count, block_customer, customer_slot, dropout_flags):
    n_dp, n_t, n_s = (lax.axis_size(n) for n in ("dp", "tensor", "sub"))
    groups = n_t * n_s
    tenants = live_token_count.shape[0]
    blocks = block_customer.shape[0]
    rows, width = x.shape
    vl = dy.shape[1]
    local_slots = down_table.shape[0]
    rk = local_slots * RANK
    onehot = (block_customer[:, None] == jnp.arange(tenants, dtype=jnp.int32)[None, :]).astype(jnp.int32)
    count = jnp.sum(onehot * live_token_count[None, :], 1)
    slot = jnp.sum(onehot * customer_slot[None, :], 1)
    tail = count - BLOCK * ((count + BLOCK - 1) // BLOCK - 1)
    ends = jnp.concatenate([block_customer[1:] != block_customer[:-1], jnp.ones((1,), bool)])
    limit = jnp.where(ends, tail, BLOCK)
    meta = jnp.stack([slot, limit, block_customer] + [slot] * 5)
    meta = jnp.broadcast_to(meta[:, :, None], (8, blocks, BLOCK)).reshape(8, rows)
    info = jnp.broadcast_to(block_customer[0], (8, BLOCK))
    shifts = jnp.arange(RANK, dtype=jnp.int32)[:, None, None] + 16 * jnp.arange(2, dtype=jnp.int32)[None, None, :]
    bits = jnp.bitwise_and(jnp.right_shift(dropout_flags[None, :, None], shifts), 1)
    drop = (2.0 * bits.astype(F32)).reshape(RANK, rows)

    vmem = pl.BlockSpec(memory_space=pltpu.VMEM)
    hbm = pl.BlockSpec(memory_space=pl.ANY)
    dma = pltpu.SemaphoreType.DMA
    all_rk = n_dp * rk
    wfull, dyfull, downall, gexp, live, sums = pl.pallas_call(
        functools.partial(exchange, (n_dp, n_t, n_s)),
        out_shape=(
            jax.ShapeDtypeStruct((groups, width, vl), BF16),
            jax.ShapeDtypeStruct((groups, rows, vl), BF16),
            jax.ShapeDtypeStruct((all_rk, width), BF16),
            jax.ShapeDtypeStruct((all_rk, rows), BF16),
            jax.ShapeDtypeStruct((8, rows), F32),
            jax.ShapeDtypeStruct((rk, width + vl), F32),
        ),
        in_specs=[hbm, vmem, hbm] + [vmem] * 5,
        out_specs=(hbm, hbm, vmem, vmem, vmem, vmem),
        scratch_shapes=[
            pltpu.VMEM((rows, width), BF16),
            pltpu.VMEM((n_dp, rk, width), BF16),
            pltpu.VMEM((n_dp, rk, vl), BF16),
            pltpu.VMEM((n_dp, 8, BLOCK), jnp.int32),
            pltpu.VMEM((2 * RANK, rows), BF16),
            pltpu.VMEM((groups, 2 * RANK, rows), BF16),
            pltpu.VMEM((n_dp, rk, width + vl), BF16),
            pltpu.VMEM((n_dp, rk, width + vl), BF16),
            dma, dma((2,)),
            dma((3, n_dp)), dma((3, n_dp)),
            dma((groups,)), dma((groups,)),
            dma((n_dp,)), dma((n_dp,)),
            dma((groups, CHUNKS)), dma((groups, CHUNKS)),
            dma((groups, CHUNKS)), dma((groups, CHUNKS)),
            dma((2, groups, CHUNKS)), dma((2, groups, CHUNKS)),
            dma, dma,
            dma((n_t,)), dma((n_t,)),
            dma((n_t,)), dma((n_t,)),
        ],
        compiler_params=pltpu.CompilerParams(
            collective_id=0, has_side_effects=True, vmem_limit_bytes=40 * 1024 * 1024
        ),
    )(x, dy, w, down_table.reshape(rk, width), up_table.reshape(rk, vl), drop, meta, info)

    tile = 256
    input_grad = pl.pallas_call(
        product,
        grid=(width // tile,),
        out_shape=jax.ShapeDtypeStruct((rows, width), BF16),
        in_specs=[
            pl.BlockSpec((groups, rows, vl), lambda j: (0, 0, 0)),
            pl.BlockSpec((groups, tile, vl), lambda j: (0, j, 0)),
            pl.BlockSpec((all_rk, tile), lambda j: (0, j)),
            pl.BlockSpec((all_rk, rows), lambda j: (0, 0)),
            pl.BlockSpec((8, rows), lambda j: (0, 0)),
        ],
        out_specs=pl.BlockSpec((rows, tile), lambda j: (0, j)),
        scratch_shapes=[pltpu.VMEM((groups, rows, vl), BF16), pltpu.VMEM((rows, all_rk), BF16)],
        compiler_params=pltpu.CompilerParams(vmem_limit_bytes=40 * 1024 * 1024),
    )(dyfull, wfull, downall, gexp, live)

    mine = lax.axis_index("dp") * local_slots + jnp.arange(local_slots, dtype=jnp.int32)
    chosen = (customer_slot[None, :] == mine[:, None]).astype(jnp.int32)
    slot_count = jnp.sum(chosen * live_token_count[None, :], 1).astype(F32)[:, None, None]
    sums = sums.reshape(local_slots, RANK, width + vl)
    return input_grad, sums[:, :, :width] / slot_count, sums[:, :, width:] / slot_count


def solution(mesh):
    return jax.shard_map(
        body,
        mesh=mesh,
        in_specs=(
            P(("parts", "dp"), ("tensor", "sub")),
            P(("parts", "dp"), ("tensor", "sub")),
            P(None, ("tensor", "sub")),
            P(("parts", "dp"), None, ("tensor", "sub")),
            P(("parts", "dp"), None, ("tensor", "sub")),
            P("parts"),
            P(("parts", "dp")),
            P("parts"),
            P(("parts", "dp")),
        ),
        out_specs=(
            P(("parts", "dp"), ("tensor", "sub")),
            P(("parts", "dp"), None, ("tensor", "sub")),
            P(("parts", "dp"), None, ("tensor", "sub")),
        ),
        check_vma=False,
    )
```

```python
import functools

import jax
import jax.numpy as jnp
from jax import lax
from jax.experimental import pallas as pl
from jax.experimental.pallas import tpu as pltpu
from jax.sharding import PartitionSpec as P

RANK = 16
BLOCK = 128
SCALE = 2.0
TILE = 256
MESH = pl.DeviceIdType.MESH
F32 = jnp.float32
BF16 = jnp.bfloat16


def dot_nt(a, b):
    return lax.dot_general(a, b, (((1,), (1,)), ((), ())), preferred_element_type=F32)


def dot_nn(a, b):
    return jnp.dot(a, b, preferred_element_type=F32)


def kernel(
    sizes,
    x_hbm, dy_hbm, w_hbm, down_hbm, up_hbm, live_count, customer, slot_of, flags_ref,
    out_ref, down_out, up_out,
    x_ref, wfull, dyfull, acc, downs, ups, info, infos, part, ranks, outgoing, incoming, keep_rows, ranked,
    own_sem, tab_send, tab_recv, rk_send, rk_recv, out_send, out_recv,
    wx_send, wx_recv, wz_send, wz_recv, wy_send, wy_recv, wd_send, wd_recv, wc_send, wc_recv,
    dx_send, dx_recv, dc_send, dc_recv,
):
    n_dp, n_t, n_s = sizes
    a, d, t, s = (lax.axis_index(n) for n in ("parts", "dp", "tensor", "sub"))
    me = t * n_s + s
    rows, width = x_ref.shape
    vl = dyfull.shape[2]
    rk = down_hbm.shape[0]
    local_slots = rk // RANK
    blocks = rows // BLOCK
    tenants = live_count.shape[0]
    quarter = width // 4
    piece = quarter // 2
    half = rows // 2
    odd = lax.rem(d, 2)
    z_peer = {"dp": d + 1 - 2 * odd}
    y_peer = {"parts": 1 - a}
    core_peer = {"sub": 1 - s}

    def ahead(dt, ds):
        return lax.rem(t + dt, n_t), lax.rem(s + ds, n_s)

    def behind(dt, ds):
        return lax.rem(t - dt + n_t, n_t), lax.rem(s - ds + n_s, n_s)

    group = [(dt, ds) for dt in range(n_t) for ds in range(n_s) if (dt, ds) != (0, 0)]
    cross = [(dt, ds) for dt, ds in group if dt]

    def remote(src, dst, send, recv, peer):
        return pltpu.make_async_remote_copy(
            src_ref=src, dst_ref=dst, send_sem=send, recv_sem=recv,
            device_id=peer, device_id_type=MESH,
        )

    barrier = pltpu.get_barrier_semaphore()
    for dt, ds in group:
        pt, ps = ahead(dt, ds)
        pl.semaphore_signal(barrier, inc=1, device_id={"tensor": pt, "sub": ps}, device_id_type=MESH)
    for off in range(1, n_dp):
        pl.semaphore_signal(barrier, inc=1, device_id={"dp": lax.rem(d + off, n_dp)}, device_id_type=MESH)
    pl.semaphore_signal(barrier, inc=1, device_id=y_peer, device_id_type=MESH)

    own_rows = pl.ds(pl.multiple_of(me * width, 16), width)
    own = [
        pltpu.make_async_copy(down_hbm, downs.at[d], own_sem.at[0]),
        pltpu.make_async_copy(up_hbm, ups.at[d], own_sem.at[1]),
        pltpu.make_async_copy(dy_hbm, dyfull.at[me], own_sem.at[2]),
        pltpu.make_async_copy(x_hbm, x_ref, own_sem.at[3]),
        pltpu.make_async_copy(w_hbm.at[own_rows], wfull.at[me], own_sem.at[4]),
    ]
    for copy in own:
        copy.start()
    info[...] = jnp.full(info.shape, customer[0], jnp.int32)

    word = flags_ref[...]
    rank_row = lax.broadcasted_iota(jnp.int32, (RANK, word.shape[1]), 0)
    word = jnp.broadcast_to(word, rank_row.shape)
    spread_row = lax.broadcasted_iota(jnp.int32, (BLOCK, 2 * BLOCK), 0)
    spread_lane = lax.broadcasted_iota(jnp.int32, (BLOCK, 2 * BLOCK), 1)
    drops = []
    for h in range(2):
        bits = jnp.bitwise_and(jnp.right_shift(word, rank_row + RANK * h), 1).astype(F32).astype(BF16)
        spread = (spread_lane == 2 * spread_row + h).astype(F32).astype(BF16)
        drops.append(jnp.concatenate(
            [dot_nn(bits[:, j * BLOCK:(j + 1) * BLOCK], spread) for j in range(rows // (2 * BLOCK))], axis=1))
    drop = 2.0 * (drops[0] + drops[1])

    slot_parts, limits = [], []
    for b in range(blocks):
        who = customer[b]
        count = live_count[who]
        tail = count - BLOCK * (jnp.right_shift(count + (BLOCK - 1), 7) - 1)
        if b + 1 < blocks:
            tail = jnp.where(customer[b + 1] == who, BLOCK, tail)
        slot_parts.append(jnp.full((1, BLOCK), slot_of[who], jnp.int32))
        limits.append(jnp.full((1, BLOCK), tail, jnp.int32))
    slot_tok = jnp.concatenate(slot_parts, axis=1)

    pl.semaphore_wait(barrier, len(group) + n_dp)
    sent = []

    def go(copy):
        copy.start()
        sent.append(copy)

    for off in range(1, n_dp):
        to = {"dp": lax.rem(d + off, n_dp)}
        go(remote(info, infos.at[off], tab_send.at[0, off], tab_recv.at[0, off], to))
        go(remote(up_hbm, ups.at[d], tab_send.at[1, off], tab_recv.at[1, off], to))
        go(remote(down_hbm, downs.at[d], tab_send.at[2, off], tab_recv.at[2, off], to))

    def span(q, c):
        return pl.ds(pl.multiple_of(q * quarter + c * piece, 16), piece)

    q_own = 2 * a + odd
    q_z = 2 * a + 1 - odd
    q_y = 2 * (1 - a) + odd
    q_yz = 2 * (1 - a) + 1 - odd
    for c in range(2):
        for dt, ds in cross:
            pt, ps = ahead(dt, ds)
            start = (pt * n_s + ps) * width + q_own * quarter + c * piece
            src = w_hbm.at[pl.ds(pl.multiple_of(start, 16), piece)]
            k = dt * n_s + ds
            go(remote(src, wfull.at[me, span(q_own, c)], wx_send.at[k, c], wx_recv.at[k, c],
                      {"tensor": pt, "sub": ps}))

    def send_dy(c):
        at = pl.ds(c * half, half)
        for dt in range(1, n_t):
            go(remote(dy_hbm.at[at], dyfull.at[me, at], dx_send.at[dt, c], dx_recv.at[dt, c],
                      {"tensor": lax.rem(t + dt, n_t)}))

    send_dy(0)
    go(remote(dy_hbm, dyfull.at[me], dc_send.at[0, 0], dc_recv.at[0, 0], core_peer))
    other_rows = pl.ds(pl.multiple_of((t * n_s + 1 - s) * width, 16), width)
    go(remote(w_hbm.at[other_rows], wfull.at[me], wc_send, wc_recv, core_peer))

    def forward(c):
        for dt, ds in cross:
            ft, fs = behind(dt, ds)
            k = dt * n_s + ds
            got = wfull.at[ft * n_s + fs, span(q_own, c)]
            remote(got, got, wx_send.at[k, c], wx_recv.at[k, c], {"tensor": ft, "sub": fs}).wait_recv()
            go(remote(got, got, wz_send.at[k, c], wz_recv.at[k, c], z_peer))
            go(remote(got, got, wy_send.at[k, c], wy_recv.at[k, c], y_peer))

    for copy in own:
        copy.wait()
    for off in range(1, n_dp):
        frm = lax.rem(d - off + n_dp, n_dp)
        here = {"dp": frm}
        remote(info, infos.at[off], tab_send.at[0, off], tab_recv.at[0, off], here).wait_recv()
        remote(up_hbm, ups.at[frm], tab_send.at[1, off], tab_recv.at[1, off], here).wait_recv()
        remote(down_hbm, downs.at[frm], tab_send.at[2, off], tab_recv.at[2, off], here).wait_recv()
    forward(0)
    slots = n_dp * local_slots
    own_slot = lax.broadcasted_iota(jnp.int32, (slots, RANK, rows), 0) == slot_tok[None]
    in_all = dot_nt(downs[...].reshape(n_dp * rk, width), x_ref[...]).reshape(slots, RANK, rows)
    grad_all = dot_nt(ups[...].reshape(n_dp * rk, vl), dyfull[me]).reshape(slots, RANK, rows)
    part[0:RANK, :] = jnp.sum(jnp.where(own_slot, in_all, 0.0), 0).astype(BF16)
    part[RANK:2 * RANK, :] = jnp.sum(jnp.where(own_slot, grad_all, 0.0), 0).astype(BF16)
    for dt, ds in group:
        pt, ps = ahead(dt, ds)
        k = dt * n_s + ds
        go(remote(part, ranks.at[me], rk_send.at[k], rk_recv.at[k], {"tensor": pt, "sub": ps}))
    send_dy(1)
    ranks[me] = part[...]

    following = infos[n_dp - 1, 0:1, :]
    goes_on = (following == customer[blocks - 1]) & (jnp.zeros_like(following) + d < n_dp - 1)
    limits[-1] = jnp.where(goes_on, BLOCK, limits[-1])
    limit = jnp.concatenate(limits, axis=1)
    lane = lax.broadcasted_iota(jnp.int32, (1, rows), 1)
    live = (jnp.bitwise_and(lane, BLOCK - 1) < limit).astype(F32)
    eye = lax.broadcasted_iota(jnp.int32, (BLOCK, BLOCK), 0) == lax.broadcasted_iota(
        jnp.int32, (BLOCK, BLOCK), 1)
    for b in range(blocks):
        at = slice(b * BLOCK, (b + 1) * BLOCK)
        column = jnp.sum(jnp.where(eye, live[:, at], 0.0), 1, keepdims=True)
        keep_rows[at, :] = jnp.broadcast_to(column, (BLOCK, BLOCK))
    forward(1)

    got = dyfull.at[t * n_s + 1 - s]
    remote(got, got, dc_send.at[0, 0], dc_recv.at[0, 0], core_peer).wait_recv()
    got = wfull.at[t * n_s + 1 - s]
    remote(got, got, wc_send, wc_recv, core_peer).wait_recv()

    @pl.loop(0, width // TILE)
    def _(j):
        at = pl.ds(pl.multiple_of(j * TILE, TILE), TILE)
        total = dot_nt(dyfull[t * n_s], wfull[t * n_s, at])
        for i in range(1, n_s):
            total += dot_nt(dyfull[t * n_s + i], wfull[t * n_s + i, at])
        acc[:, at] = total

    for dt, ds in group:
        ft, fs = behind(dt, ds)
        k = dt * n_s + ds
        remote(part, ranks.at[ft * n_s + fs], rk_send.at[k], rk_recv.at[k],
               {"tensor": ft, "sub": fs}).wait_recv()
    total = jnp.sum(ranks[...].astype(F32), 0)
    keep = drop * (SCALE * live)
    dropped = total[0:RANK] * keep
    grad_rank = total[RANK:2 * RANK] * keep
    dropped_all = jnp.where(own_slot, dropped[None], 0.0).reshape(n_dp * rk, rows).astype(BF16)
    grad_all = jnp.where(own_slot, grad_rank[None], 0.0).reshape(n_dp * rk, rows)
    up_part = dot_nn(dropped_all, dyfull[me])
    outgoing[:, :, width:] = up_part.reshape(n_dp, rk, vl).astype(BF16)
    down_part = dot_nn(grad_all.astype(BF16), x_ref[...])
    outgoing[:, :, :width] = down_part.reshape(n_dp, rk, width).astype(BF16)
    for off in range(1, n_dp):
        to = lax.rem(d + off, n_dp)
        go(remote(outgoing.at[to], incoming.at[off], out_send.at[off], out_recv.at[off], {"dp": to}))
    incoming[0] = outgoing[d]
    ranked[...] = grad_all.T.astype(BF16)

    for dt, ds in cross:
        ft, fs = behind(dt, ds)
        g = ft * n_s + fs
        k = dt * n_s + ds
        got = wfull.at[g, span(q_z, 0)]
        remote(got, got, wz_send.at[k, 0], wz_recv.at[k, 0], z_peer).wait_recv()
        go(remote(got, got, wd_send.at[k, 0], wd_recv.at[k, 0], y_peer))
        for c in range(2):
            got = wfull.at[g, span(q_y, c)]
            remote(got, got, wy_send.at[k, c], wy_recv.at[k, c], y_peer).wait_recv()
        go(remote(got, got, wd_send.at[k, 1], wd_recv.at[k, 1], z_peer))
    for c in range(2):
        at = pl.ds(c * half, half)
        for dt in range(1, n_t):
            ft = lax.rem(t - dt + n_t, n_t)
            got = dyfull.at[ft * n_s + s, at]
            remote(got, got, dx_send.at[dt, c], dx_recv.at[dt, c], {"tensor": ft}).wait_recv()
            go(remote(got, got, dc_send.at[dt, c], dc_recv.at[dt, c], core_peer))
    for c in range(2):
        at = pl.ds(c * half, half)
        for dt in range(1, n_t):
            got = dyfull.at[lax.rem(t - dt + n_t, n_t) * n_s + 1 - s, at]
            remote(got, got, dc_send.at[dt, c], dc_recv.at[dt, c], core_peer).wait_recv()

    def finish(q):
        @pl.loop(0, quarter // TILE)
        def _(j):
            at = pl.ds(pl.multiple_of(q * quarter + j * TILE, TILE), TILE)
            total = acc[:, at] + dot_nn(ranked[...], downs[:, :, at].reshape(n_dp * rk, TILE))
            for dt in range(1, n_t):
                for i in range(n_s):
                    g = lax.rem(t + dt, n_t) * n_s + i
                    total += dot_nt(dyfull[g], wfull[g, at])
            live_row = jnp.concatenate([keep_rows[...]] * (TILE // BLOCK), axis=1)
            out_ref[:, at] = jnp.where(live_row > 0, total, 0.0).astype(BF16)

    finish(q_own)
    for dt, ds in cross:
        ft, fs = behind(dt, ds)
        k = dt * n_s + ds
        got = wfull.at[ft * n_s + fs, span(q_z, 1)]
        remote(got, got, wz_send.at[k, 1], wz_recv.at[k, 1], z_peer).wait_recv()
    finish(q_z)
    finish(q_y)

    for off in range(1, n_dp):
        remote(outgoing.at[d], incoming.at[off], out_send.at[off], out_recv.at[off],
               {"dp": lax.rem(d - off + n_dp, n_dp)}).wait_recv()
    for j in range(local_slots):
        at = slice(j * RANK, (j + 1) * RANK)
        count = 0
        for tenant in range(tenants):
            count += jnp.where(slot_of[tenant] == d * local_slots + j, live_count[tenant], 0)
        sums = jnp.sum(incoming[:, at, :].astype(F32), 0)
        sums = sums / jnp.full((1, width + vl), count, jnp.int32).astype(F32)
        down_out[at, :] = sums[:, :width]
        up_out[at, :] = sums[:, width:]

    for dt, ds in cross:
        ft, fs = behind(dt, ds)
        g = ft * n_s + fs
        k = dt * n_s + ds
        for c, peer in enumerate((y_peer, z_peer)):
            got = wfull.at[g, span(q_yz, c)]
            remote(got, got, wd_send.at[k, c], wd_recv.at[k, c], peer).wait_recv()
    finish(q_yz)
    for copy in sent:
        copy.wait_send()


def body(x, dy, w, down_table, up_table, live_token_count, block_customer, customer_slot, dropout_flags):
    n_dp, n_t, n_s = (lax.axis_size(n) for n in ("dp", "tensor", "sub"))
    groups = n_t * n_s
    rows, width = x.shape
    vl = dy.shape[1]
    local_slots = down_table.shape[0]
    rk = local_slots * RANK
    all_rk = n_dp * rk
    vmem = pl.BlockSpec(memory_space=pltpu.VMEM)
    smem = pl.BlockSpec(memory_space=pltpu.SMEM)
    hbm = pl.BlockSpec(memory_space=pltpu.HBM)
    dma = pltpu.SemaphoreType.DMA
    input_grad, down_grad, up_grad = pl.pallas_call(
        functools.partial(kernel, (n_dp, n_t, n_s)),
        out_shape=(
            jax.ShapeDtypeStruct((rows, width), BF16),
            jax.ShapeDtypeStruct((rk, width), F32),
            jax.ShapeDtypeStruct((rk, vl), F32),
        ),
        in_specs=[hbm] * 5 + [smem] * 3 + [vmem],
        out_specs=(vmem, vmem, vmem),
        scratch_shapes=[
            pltpu.VMEM((rows, width), BF16),
            pltpu.VMEM((groups, width, vl), BF16),
            pltpu.VMEM((groups, rows, vl), BF16),
            pltpu.VMEM((rows, width), F32),
            pltpu.VMEM((n_dp, rk, width), BF16),
            pltpu.VMEM((n_dp, rk, vl), BF16),
            pltpu.VMEM((8, BLOCK), jnp.int32),
            pltpu.VMEM((n_dp, 8, BLOCK), jnp.int32),
            pltpu.VMEM((2 * RANK, rows), BF16),
            pltpu.VMEM((groups, 2 * RANK, rows), BF16),
            pltpu.VMEM((n_dp, rk, width + vl), BF16),
            pltpu.VMEM((n_dp, rk, width + vl), BF16),
            pltpu.VMEM((rows, BLOCK), F32),
            pltpu.VMEM((rows, all_rk), BF16),
            dma((5,)),
            dma((3, n_dp)), dma((3, n_dp)),
            dma((groups,)), dma((groups,)),
            dma((n_dp,)), dma((n_dp,)),
            dma((groups, 2)), dma((groups, 2)),
            dma((groups, 2)), dma((groups, 2)),
            dma((groups, 2)), dma((groups, 2)),
            dma((groups, 2)), dma((groups, 2)),
            dma, dma,
            dma((n_t, 2)), dma((n_t, 2)),
            dma((n_t, 2)), dma((n_t, 2)),
        ],
        compiler_params=pltpu.CompilerParams(
            collective_id=0, has_side_effects=True, vmem_limit_bytes=48 * 1024 * 1024
        ),
    )(x, dy, w, down_table.reshape(rk, width), up_table.reshape(rk, vl),
      live_token_count, block_customer, customer_slot, dropout_flags.reshape(1, -1))
    return input_grad, down_grad.reshape(local_slots, RANK, width), up_grad.reshape(local_slots, RANK, vl)


def solution(mesh):
    return jax.shard_map(
        body,
        mesh=mesh,
        in_specs=(
            P(("parts", "dp"), ("tensor", "sub")),
            P(("parts", "dp"), ("tensor", "sub")),
            P(None, ("tensor", "sub")),
            P(("parts", "dp"), None, ("tensor", "sub")),
            P(("parts", "dp"), None, ("tensor", "sub")),
            P("parts"),
            P(("parts", "dp")),
            P("parts"),
            P(("parts", "dp")),
        ),
        out_specs=(
            P(("parts", "dp"), ("tensor", "sub")),
            P(("parts", "dp"), None, ("tensor", "sub")),
            P(("parts", "dp"), None, ("tensor", "sub")),
        ),
        check_vma=False,
    )
```

```python
import functools

import jax
import jax.numpy as jnp
from jax import lax
from jax.experimental import pallas as pl
from jax.experimental.pallas import tpu as pltpu
from jax.sharding import PartitionSpec as P

RANK = 16
BLOCK = 128
SCALE = 2.0
TILE = 256
PIECES = 4
OVER_Y = 3
MESH = pl.DeviceIdType.MESH
F32 = jnp.float32
BF16 = jnp.bfloat16


def stay(array):
    return pltpu.with_memory_space_constraint(array, pltpu.HBM)


def dot_nt(a, b):
    return lax.dot_general(a, b, (((1,), (1,)), ((), ())), preferred_element_type=F32)


def dot_nn(a, b):
    return jnp.dot(a, b, preferred_element_type=F32)


def kernel(
    sizes,
    x_hbm, dy_hbm, w_hbm, down_hbm, up_hbm, live_count, customer, slot_of, flags_ref,
    out_ref, down_out, up_out,
    x_ref, wfull, dyfull, acc, downs, ups, info, infos, part, ranks, outgoing, incoming, keep_rows, ranked,
    own_sem, tab_send, tab_recv, rk_send, rk_recv, out_send, out_recv,
    wx_send, wx_recv, wz_send, wz_recv, wy_send, wy_recv, wd_send, wd_recv, wc_send, wc_recv,
    dx_send, dx_recv, dc_send, dc_recv,
):
    n_dp, n_t, n_s = sizes
    a, d, t, s = (lax.axis_index(n) for n in ("parts", "dp", "tensor", "sub"))
    me = t * n_s + s
    rows, width = x_ref.shape
    vl = dyfull.shape[2]
    rk = down_hbm.shape[0]
    local_slots = rk // RANK
    blocks = rows // BLOCK
    tenants = live_count.shape[0]
    quarter = width // 4
    piece = quarter // PIECES
    half = rows // 2
    odd = lax.rem(d, 2)
    z_peer = {"dp": d + 1 - 2 * odd}
    y_peer = {"parts": 1 - a}
    core_peer = {"sub": 1 - s}

    def ahead(dt, ds):
        return lax.rem(t + dt, n_t), lax.rem(s + ds, n_s)

    def behind(dt, ds):
        return lax.rem(t - dt + n_t, n_t), lax.rem(s - ds + n_s, n_s)

    group = [(dt, ds) for dt in range(n_t) for ds in range(n_s) if (dt, ds) != (0, 0)]
    cross = [(dt, ds) for dt, ds in group if dt]

    def remote(src, dst, send, recv, peer):
        return pltpu.make_async_remote_copy(
            src_ref=src, dst_ref=dst, send_sem=send, recv_sem=recv,
            device_id=peer, device_id_type=MESH,
        )

    barrier = pltpu.get_barrier_semaphore()
    for dt, ds in group:
        pt, ps = ahead(dt, ds)
        pl.semaphore_signal(barrier, inc=1, device_id={"tensor": pt, "sub": ps}, device_id_type=MESH)
    for off in range(1, n_dp):
        pl.semaphore_signal(barrier, inc=1, device_id={"dp": lax.rem(d + off, n_dp)}, device_id_type=MESH)
    pl.semaphore_signal(barrier, inc=1, device_id=y_peer, device_id_type=MESH)

    own_rows = pl.ds(pl.multiple_of(me * width, 16), width)
    own = [
        pltpu.make_async_copy(down_hbm, downs.at[d], own_sem.at[0]),
        pltpu.make_async_copy(up_hbm, ups.at[d], own_sem.at[1]),
        pltpu.make_async_copy(dy_hbm, dyfull.at[me], own_sem.at[2]),
        pltpu.make_async_copy(x_hbm, x_ref, own_sem.at[3]),
        pltpu.make_async_copy(w_hbm.at[own_rows], wfull.at[me], own_sem.at[4]),
    ]
    for copy in own:
        copy.start()
    info[...] = jnp.full(info.shape, customer[0], jnp.int32)

    word = flags_ref[...]
    rank_row = lax.broadcasted_iota(jnp.int32, (RANK, word.shape[1]), 0)
    word = jnp.broadcast_to(word, rank_row.shape)
    spread_row = lax.broadcasted_iota(jnp.int32, (BLOCK, 2 * BLOCK), 0)
    spread_lane = lax.broadcasted_iota(jnp.int32, (BLOCK, 2 * BLOCK), 1)
    drops = []
    for h in range(2):
        bits = jnp.bitwise_and(jnp.right_shift(word, rank_row + RANK * h), 1).astype(F32).astype(BF16)
        spread = (spread_lane == 2 * spread_row + h).astype(F32).astype(BF16)
        drops.append(jnp.concatenate(
            [dot_nn(bits[:, j * BLOCK:(j + 1) * BLOCK], spread) for j in range(rows // (2 * BLOCK))], axis=1))
    drop = 2.0 * (drops[0] + drops[1])

    slot_parts, limits = [], []
    for b in range(blocks):
        who = customer[b]
        count = live_count[who]
        tail = count - BLOCK * (jnp.right_shift(count + (BLOCK - 1), 7) - 1)
        if b + 1 < blocks:
            tail = jnp.where(customer[b + 1] == who, BLOCK, tail)
        slot_parts.append(jnp.full((1, BLOCK), slot_of[who], jnp.int32))
        limits.append(jnp.full((1, BLOCK), tail, jnp.int32))
    slot_tok = jnp.concatenate(slot_parts, axis=1)

    pl.semaphore_wait(barrier, len(group) + n_dp)
    sent = []

    def go(copy):
        copy.start()
        sent.append(copy)

    for off in range(1, n_dp):
        to = {"dp": lax.rem(d + off, n_dp)}
        go(remote(info, infos.at[off], tab_send.at[0, off], tab_recv.at[0, off], to))
        go(remote(up_hbm, ups.at[d], tab_send.at[1, off], tab_recv.at[1, off], to))
        go(remote(down_hbm, downs.at[d], tab_send.at[2, off], tab_recv.at[2, off], to))

    def span(q, c):
        return pl.ds(pl.multiple_of(q * quarter + c * piece, 16), piece)

    q_own = 2 * a + odd
    q_z = 2 * a + 1 - odd
    q_y = 2 * (1 - a) + odd
    q_yz = 2 * (1 - a) + 1 - odd
    for c in range(PIECES):
        for dt, ds in cross:
            pt, ps = ahead(dt, ds)
            start = (pt * n_s + ps) * width + q_own * quarter + c * piece
            src = w_hbm.at[pl.ds(pl.multiple_of(start, 16), piece)]
            k = dt * n_s + ds
            go(remote(src, wfull.at[me, span(q_own, c)], wx_send.at[k, c], wx_recv.at[k, c],
                      {"tensor": pt, "sub": ps}))

    def send_dy(c):
        at = pl.ds(c * half, half)
        for dt in range(1, n_t):
            go(remote(dy_hbm.at[at], dyfull.at[me, at], dx_send.at[dt, c], dx_recv.at[dt, c],
                      {"tensor": lax.rem(t + dt, n_t)}))

    go(remote(dy_hbm, dyfull.at[me], dc_send.at[0, 0], dc_recv.at[0, 0], core_peer))
    other_rows = pl.ds(pl.multiple_of((t * n_s + 1 - s) * width, 16), width)
    go(remote(w_hbm.at[other_rows], wfull.at[me], wc_send, wc_recv, core_peer))

    def forward(c):
        for dt, ds in cross:
            ft, fs = behind(dt, ds)
            k = dt * n_s + ds
            got = wfull.at[ft * n_s + fs, span(q_own, c)]
            remote(got, got, wx_send.at[k, c], wx_recv.at[k, c], {"tensor": ft, "sub": fs}).wait_recv()
            go(remote(got, got, wz_send.at[k, c], wz_recv.at[k, c], z_peer))
            go(remote(got, got, wy_send.at[k, c], wy_recv.at[k, c], y_peer))

    for c in range(PIECES // 2):
        forward(c)
    for copy in own:
        copy.wait()
    for off in range(1, n_dp):
        frm = lax.rem(d - off + n_dp, n_dp)
        here = {"dp": frm}
        remote(info, infos.at[off], tab_send.at[0, off], tab_recv.at[0, off], here).wait_recv()
        remote(up_hbm, ups.at[frm], tab_send.at[1, off], tab_recv.at[1, off], here).wait_recv()
        remote(down_hbm, downs.at[frm], tab_send.at[2, off], tab_recv.at[2, off], here).wait_recv()
    slots = n_dp * local_slots
    own_slot = lax.broadcasted_iota(jnp.int32, (slots, RANK, rows), 0) == slot_tok[None]
    in_all = dot_nt(downs[...].reshape(n_dp * rk, width), x_ref[...]).reshape(slots, RANK, rows)
    grad_all = dot_nt(ups[...].reshape(n_dp * rk, vl), dyfull[me]).reshape(slots, RANK, rows)
    part[0:RANK, :] = jnp.sum(jnp.where(own_slot, in_all, 0.0), 0).astype(BF16)
    part[RANK:2 * RANK, :] = jnp.sum(jnp.where(own_slot, grad_all, 0.0), 0).astype(BF16)
    for dt, ds in group:
        pt, ps = ahead(dt, ds)
        k = dt * n_s + ds
        go(remote(part, ranks.at[me], rk_send.at[k], rk_recv.at[k], {"tensor": pt, "sub": ps}))
    for c in range(2):
        send_dy(c)
    for c in range(PIECES // 2, PIECES):
        forward(c)
    ranks[me] = part[...]

    following = infos[n_dp - 1, 0:1, :]
    goes_on = (following == customer[blocks - 1]) & (jnp.zeros_like(following) + d < n_dp - 1)
    limits[-1] = jnp.where(goes_on, BLOCK, limits[-1])
    limit = jnp.concatenate(limits, axis=1)
    lane = lax.broadcasted_iota(jnp.int32, (1, rows), 1)
    live = (jnp.bitwise_and(lane, BLOCK - 1) < limit).astype(F32)
    eye = lax.broadcasted_iota(jnp.int32, (BLOCK, BLOCK), 0) == lax.broadcasted_iota(
        jnp.int32, (BLOCK, BLOCK), 1)
    for b in range(blocks):
        at = slice(b * BLOCK, (b + 1) * BLOCK)
        column = jnp.sum(jnp.where(eye, live[:, at], 0.0), 1, keepdims=True)
        keep_rows[at, :] = jnp.broadcast_to(column, (BLOCK, BLOCK))

    got = dyfull.at[t * n_s + 1 - s]
    remote(got, got, dc_send.at[0, 0], dc_recv.at[0, 0], core_peer).wait_recv()
    got = wfull.at[t * n_s + 1 - s]
    remote(got, got, wc_send, wc_recv, core_peer).wait_recv()

    @pl.loop(0, width // TILE)
    def _(j):
        at = pl.ds(pl.multiple_of(j * TILE, TILE), TILE)
        total = dot_nt(dyfull[t * n_s], wfull[t * n_s, at])
        for i in range(1, n_s):
            total += dot_nt(dyfull[t * n_s + i], wfull[t * n_s + i, at])
        acc[:, at] = total

    for dt, ds in group:
        ft, fs = behind(dt, ds)
        k = dt * n_s + ds
        remote(part, ranks.at[ft * n_s + fs], rk_send.at[k], rk_recv.at[k],
               {"tensor": ft, "sub": fs}).wait_recv()
    total = jnp.sum(ranks[...].astype(F32), 0)
    keep = drop * (SCALE * live)
    dropped = total[0:RANK] * keep
    grad_rank = total[RANK:2 * RANK] * keep
    dropped_all = jnp.where(own_slot, dropped[None], 0.0).reshape(n_dp * rk, rows).astype(BF16)
    grad_all = jnp.where(own_slot, grad_rank[None], 0.0).reshape(n_dp * rk, rows)
    up_part = dot_nn(dropped_all, dyfull[me])
    outgoing[:, :, width:] = up_part.reshape(n_dp, rk, vl).astype(BF16)
    down_part = dot_nn(grad_all.astype(BF16), x_ref[...])
    outgoing[:, :, :width] = down_part.reshape(n_dp, rk, width).astype(BF16)
    for off in range(1, n_dp):
        to = lax.rem(d + off, n_dp)
        go(remote(outgoing.at[to], incoming.at[off], out_send.at[off], out_recv.at[off], {"dp": to}))
    incoming[0] = outgoing[d]
    ranked[...] = grad_all.T.astype(BF16)

    for dt, ds in cross:
        ft, fs = behind(dt, ds)
        g = ft * n_s + fs
        k = dt * n_s + ds
        for c in range(PIECES):
            got_z = wfull.at[g, span(q_z, c)]
            remote(got_z, got_z, wz_send.at[k, c], wz_recv.at[k, c], z_peer).wait_recv()
            got_y = wfull.at[g, span(q_y, c)]
            remote(got_y, got_y, wy_send.at[k, c], wy_recv.at[k, c], y_peer).wait_recv()
            got, peer = (got_z, y_peer) if c < OVER_Y else (got_y, z_peer)
            go(remote(got, got, wd_send.at[k, c], wd_recv.at[k, c], peer))

    def pass_on(c):
        at = pl.ds(c * half, half)
        for dt in range(1, n_t):
            ft = lax.rem(t - dt + n_t, n_t)
            got = dyfull.at[ft * n_s + s, at]
            remote(got, got, dx_send.at[dt, c], dx_recv.at[dt, c], {"tensor": ft}).wait_recv()
            go(remote(got, got, dc_send.at[dt, c], dc_recv.at[dt, c], core_peer))
        for dt in range(1, n_t):
            got = dyfull.at[lax.rem(t - dt + n_t, n_t) * n_s + 1 - s, at]
            remote(got, got, dc_send.at[dt, c], dc_recv.at[dt, c], core_peer).wait_recv()

    def finish(c, q):
        high = pl.ds(c * half, half)

        @pl.loop(0, quarter // TILE)
        def _(j):
            at = pl.ds(pl.multiple_of(q * quarter + j * TILE, TILE), TILE)
            total = acc[high, at] + dot_nn(ranked[high, :], downs[:, :, at].reshape(n_dp * rk, TILE))
            for dt in range(1, n_t):
                for i in range(n_s):
                    g = lax.rem(t + dt, n_t) * n_s + i
                    total += dot_nt(dyfull[g, high, :], wfull[g, at])
            live_row = jnp.concatenate([keep_rows[high, :]] * (TILE // BLOCK), axis=1)
            out_ref[high, at] = jnp.where(live_row > 0, total, 0.0).astype(BF16)

    pass_on(0)
    for q in (q_own, q_z, q_y):
        finish(0, q)

    for off in range(1, n_dp):
        remote(outgoing.at[d], incoming.at[off], out_send.at[off], out_recv.at[off],
               {"dp": lax.rem(d - off + n_dp, n_dp)}).wait_recv()
    for j in range(local_slots):
        at = slice(j * RANK, (j + 1) * RANK)
        count = 0
        for tenant in range(tenants):
            count += jnp.where(slot_of[tenant] == d * local_slots + j, live_count[tenant], 0)
        sums = jnp.sum(incoming[:, at, :].astype(F32), 0)
        sums = sums / jnp.full((1, width + vl), count, jnp.int32).astype(F32)
        down_out[at, :] = sums[:, :width]
        up_out[at, :] = sums[:, width:]

    for dt, ds in cross:
        ft, fs = behind(dt, ds)
        g = ft * n_s + fs
        k = dt * n_s + ds
        for c in range(PIECES):
            got = wfull.at[g, span(q_yz, c)]
            remote(got, got, wd_send.at[k, c], wd_recv.at[k, c], y_peer if c < OVER_Y else z_peer).wait_recv()
    finish(0, q_yz)
    pass_on(1)
    for q in (q_own, q_z, q_y, q_yz):
        finish(1, q)
    for copy in sent:
        copy.wait_send()


def body(x, dy, w, down_table, up_table, live_token_count, block_customer, customer_slot, dropout_flags):
    n_dp, n_t, n_s = (lax.axis_size(n) for n in ("dp", "tensor", "sub"))
    groups = n_t * n_s
    rows, width = x.shape
    vl = dy.shape[1]
    local_slots = down_table.shape[0]
    rk = local_slots * RANK
    all_rk = n_dp * rk
    vmem = pl.BlockSpec(memory_space=pltpu.VMEM)
    smem = pl.BlockSpec(memory_space=pltpu.SMEM)
    hbm = pl.BlockSpec(memory_space=pltpu.HBM)
    dma = pltpu.SemaphoreType.DMA
    input_grad, down_grad, up_grad = pl.pallas_call(
        functools.partial(kernel, (n_dp, n_t, n_s)),
        out_shape=(
            jax.ShapeDtypeStruct((rows, width), BF16),
            jax.ShapeDtypeStruct((rk, width), F32),
            jax.ShapeDtypeStruct((rk, vl), F32),
        ),
        in_specs=[hbm] * 5 + [smem] * 3 + [vmem],
        out_specs=(vmem, vmem, vmem),
        scratch_shapes=[
            pltpu.VMEM((rows, width), BF16),
            pltpu.VMEM((groups, width, vl), BF16),
            pltpu.VMEM((groups, rows, vl), BF16),
            pltpu.VMEM((rows, width), F32),
            pltpu.VMEM((n_dp, rk, width), BF16),
            pltpu.VMEM((n_dp, rk, vl), BF16),
            pltpu.VMEM((8, BLOCK), jnp.int32),
            pltpu.VMEM((n_dp, 8, BLOCK), jnp.int32),
            pltpu.VMEM((2 * RANK, rows), BF16),
            pltpu.VMEM((groups, 2 * RANK, rows), BF16),
            pltpu.VMEM((n_dp, rk, width + vl), BF16),
            pltpu.VMEM((n_dp, rk, width + vl), BF16),
            pltpu.VMEM((rows, BLOCK), F32),
            pltpu.VMEM((rows, all_rk), BF16),
            dma((5,)),
            dma((3, n_dp)), dma((3, n_dp)),
            dma((groups,)), dma((groups,)),
            dma((n_dp,)), dma((n_dp,)),
            dma((groups, PIECES)), dma((groups, PIECES)),
            dma((groups, PIECES)), dma((groups, PIECES)),
            dma((groups, PIECES)), dma((groups, PIECES)),
            dma((groups, PIECES)), dma((groups, PIECES)),
            dma, dma,
            dma((n_t, 2)), dma((n_t, 2)),
            dma((n_t, 2)), dma((n_t, 2)),
        ],
        compiler_params=pltpu.CompilerParams(
            collective_id=0, has_side_effects=True, vmem_limit_bytes=48 * 1024 * 1024
        ),
    )(x, stay(dy), w, stay(down_table.reshape(rk, width)), stay(up_table.reshape(rk, vl)),
      stay(live_token_count), stay(block_customer), stay(customer_slot), stay(dropout_flags.reshape(1, -1)))
    return input_grad, down_grad.reshape(local_slots, RANK, width), up_grad.reshape(local_slots, RANK, vl)


def solution(mesh):
    return jax.shard_map(
        body,
        mesh=mesh,
        in_specs=(
            P(("parts", "dp"), ("tensor", "sub")),
            P(("parts", "dp"), ("tensor", "sub")),
            P(None, ("tensor", "sub")),
            P(("parts", "dp"), None, ("tensor", "sub")),
            P(("parts", "dp"), None, ("tensor", "sub")),
            P("parts"),
            P(("parts", "dp")),
            P("parts"),
            P(("parts", "dp")),
        ),
        out_specs=(
            P(("parts", "dp"), ("tensor", "sub")),
            P(("parts", "dp"), None, ("tensor", "sub")),
            P(("parts", "dp"), None, ("tensor", "sub")),
        ),
        check_vma=False,
    )
```

```python
import functools

import jax
import jax.numpy as jnp
from jax import lax
from jax.experimental import pallas as pl
from jax.experimental.pallas import tpu as pltpu
from jax.sharding import PartitionSpec as P

RANK = 16
BLOCK = 128
SCALE = 2.0
PIECES = 4
OVER_Y = 3
STAGES = ((0, 2), (2, 3), (3, 4))
MESH = pl.DeviceIdType.MESH
F32 = jnp.float32
BF16 = jnp.bfloat16


def stay(array):
    return pltpu.with_memory_space_constraint(array, pltpu.HBM)


def dot_nt(a, b):
    return lax.dot_general(a, b, (((1,), (1,)), ((), ())), preferred_element_type=F32)


def dot_nn(a, b):
    return jnp.dot(a, b, preferred_element_type=F32)


def kernel(
    sizes,
    x_hbm, dy_hbm, w_hbm, down_hbm, up_hbm, live_count, customer, slot_of, flags_ref,
    out_ref, down_out, up_out,
    x_ref, wfull, dyfull, acc, downs, ups, info, infos, part, ranks, outgoing, incoming, keep_rows, ranked,
    own_sem, tab_send, tab_recv, rk_send, rk_recv, out_send, out_recv,
    wx_send, wx_recv, wz_send, wz_recv, wy_send, wy_recv, wd_send, wd_recv, wc_send, wc_recv,
    dx_send, dx_recv, dc_send, dc_recv,
):
    n_dp, n_t, n_s = sizes
    a, d, t, s = (lax.axis_index(n) for n in ("parts", "dp", "tensor", "sub"))
    me = t * n_s + s
    rows, width = x_ref.shape
    vl = up_hbm.shape[1]
    rk = down_hbm.shape[0]
    local_slots = rk // RANK
    blocks = rows // BLOCK
    tenants = live_count.shape[0]
    quarter = width // 4
    piece = quarter // PIECES
    share = rows // PIECES
    odd = lax.rem(d, 2)
    z_peer = {"dp": d + 1 - 2 * odd}
    y_peer = {"parts": 1 - a}
    core_peer = {"sub": 1 - s}

    def ahead(dt, ds):
        return lax.rem(t + dt, n_t), lax.rem(s + ds, n_s)

    def behind(dt, ds):
        return lax.rem(t - dt + n_t, n_t), lax.rem(s - ds + n_s, n_s)

    def cols(g):
        return pl.ds(pl.multiple_of(g * vl, BLOCK), vl)

    def chip_cols(tt):
        return pl.ds(pl.multiple_of(tt * n_s * vl, BLOCK), n_s * vl)

    group = [(dt, ds) for dt in range(n_t) for ds in range(n_s) if (dt, ds) != (0, 0)]
    cross = [(dt, ds) for dt, ds in group if dt]

    def remote(src, dst, send, recv, peer):
        return pltpu.make_async_remote_copy(
            src_ref=src, dst_ref=dst, send_sem=send, recv_sem=recv,
            device_id=peer, device_id_type=MESH,
        )

    barrier = pltpu.get_barrier_semaphore()
    for dt, ds in group:
        pt, ps = ahead(dt, ds)
        pl.semaphore_signal(barrier, inc=1, device_id={"tensor": pt, "sub": ps}, device_id_type=MESH)
    for off in range(1, n_dp):
        pl.semaphore_signal(barrier, inc=1, device_id={"dp": lax.rem(d + off, n_dp)}, device_id_type=MESH)
    pl.semaphore_signal(barrier, inc=1, device_id=y_peer, device_id_type=MESH)

    own_rows = pl.ds(pl.multiple_of(me * width, 16), width)
    own = [
        pltpu.make_async_copy(down_hbm, downs.at[d], own_sem.at[0]),
        pltpu.make_async_copy(up_hbm, ups.at[d], own_sem.at[1]),
        pltpu.make_async_copy(dy_hbm, dyfull.at[:, cols(me)], own_sem.at[2]),
        pltpu.make_async_copy(x_hbm, x_ref, own_sem.at[3]),
        pltpu.make_async_copy(w_hbm.at[own_rows], wfull.at[:, cols(me)], own_sem.at[4]),
    ]
    for copy in own:
        copy.start()
    info[...] = jnp.full(info.shape, customer[0], jnp.int32)

    word = flags_ref[...]
    rank_row = lax.broadcasted_iota(jnp.int32, (RANK, word.shape[1]), 0)
    word = jnp.broadcast_to(word, rank_row.shape)
    spread_row = lax.broadcasted_iota(jnp.int32, (BLOCK, 2 * BLOCK), 0)
    spread_lane = lax.broadcasted_iota(jnp.int32, (BLOCK, 2 * BLOCK), 1)
    drops = []
    for h in range(2):
        bits = jnp.bitwise_and(jnp.right_shift(word, rank_row + RANK * h), 1).astype(F32).astype(BF16)
        spread = (spread_lane == 2 * spread_row + h).astype(F32).astype(BF16)
        drops.append(jnp.concatenate(
            [dot_nn(bits[:, j * BLOCK:(j + 1) * BLOCK], spread) for j in range(rows // (2 * BLOCK))], axis=1))
    drop = 2.0 * (drops[0] + drops[1])

    slot_parts, limits = [], []
    for b in range(blocks):
        who = customer[b]
        count = live_count[who]
        tail = count - BLOCK * (jnp.right_shift(count + (BLOCK - 1), 7) - 1)
        if b + 1 < blocks:
            tail = jnp.where(customer[b + 1] == who, BLOCK, tail)
        slot_parts.append(jnp.full((1, BLOCK), slot_of[who], jnp.int32))
        limits.append(jnp.full((1, BLOCK), tail, jnp.int32))
    slot_tok = jnp.concatenate(slot_parts, axis=1)

    pl.semaphore_wait(barrier, len(group) + n_dp)
    sent = []

    def go(copy):
        copy.start()
        sent.append(copy)

    for off in range(1, n_dp):
        to = {"dp": lax.rem(d + off, n_dp)}
        go(remote(info, infos.at[off], tab_send.at[0, off], tab_recv.at[0, off], to))
        go(remote(up_hbm, ups.at[d], tab_send.at[1, off], tab_recv.at[1, off], to))
        go(remote(down_hbm, downs.at[d], tab_send.at[2, off], tab_recv.at[2, off], to))

    def span(q, c):
        return pl.ds(pl.multiple_of(q * quarter + c * piece, 16), piece)

    q_own = 2 * a + odd
    q_z = 2 * a + 1 - odd
    q_y = 2 * (1 - a) + odd
    q_yz = 2 * (1 - a) + 1 - odd
    for c in range(PIECES):
        for dt, ds in cross:
            pt, ps = ahead(dt, ds)
            start = (pt * n_s + ps) * width + q_own * quarter + c * piece
            src = w_hbm.at[pl.ds(pl.multiple_of(start, 16), piece)]
            k = dt * n_s + ds
            go(remote(src, wfull.at[span(q_own, c), cols(me)], wx_send.at[k, c], wx_recv.at[k, c],
                      {"tensor": pt, "sub": ps}))

    def send_dy(c):
        at = pl.ds(c * share, share)
        for dt in range(1, n_t):
            go(remote(dy_hbm.at[at], dyfull.at[at, cols(me)], dx_send.at[dt, c], dx_recv.at[dt, c],
                      {"tensor": lax.rem(t + dt, n_t)}))

    go(remote(dy_hbm, dyfull.at[:, cols(me)], dc_send.at[0, 0], dc_recv.at[0, 0], core_peer))
    other_rows = pl.ds(pl.multiple_of((t * n_s + 1 - s) * width, 16), width)
    go(remote(w_hbm.at[other_rows], wfull.at[:, cols(me)], wc_send, wc_recv, core_peer))

    def forward(c):
        for dt, ds in cross:
            ft, fs = behind(dt, ds)
            k = dt * n_s + ds
            got = wfull.at[span(q_own, c), cols(ft * n_s + fs)]
            remote(got, got, wx_send.at[k, c], wx_recv.at[k, c], {"tensor": ft, "sub": fs}).wait_recv()
            go(remote(got, got, wz_send.at[k, c], wz_recv.at[k, c], z_peer))
            go(remote(got, got, wy_send.at[k, c], wy_recv.at[k, c], y_peer))

    for c in range(PIECES // 2):
        forward(c)
    for copy in own:
        copy.wait()
    for off in range(1, n_dp):
        frm = lax.rem(d - off + n_dp, n_dp)
        here = {"dp": frm}
        remote(info, infos.at[off], tab_send.at[0, off], tab_recv.at[0, off], here).wait_recv()
        remote(up_hbm, ups.at[frm], tab_send.at[1, off], tab_recv.at[1, off], here).wait_recv()
        remote(down_hbm, downs.at[frm], tab_send.at[2, off], tab_recv.at[2, off], here).wait_recv()
    slots = n_dp * local_slots
    own_slot = lax.broadcasted_iota(jnp.int32, (slots, RANK, rows), 0) == slot_tok[None]
    in_all = dot_nt(downs[...].reshape(n_dp * rk, width), x_ref[...]).reshape(slots, RANK, rows)
    grad_all = dot_nt(ups[...].reshape(n_dp * rk, vl), dyfull[:, cols(me)]).reshape(slots, RANK, rows)
    part[0:RANK, :] = jnp.sum(jnp.where(own_slot, in_all, 0.0), 0).astype(BF16)
    part[RANK:2 * RANK, :] = jnp.sum(jnp.where(own_slot, grad_all, 0.0), 0).astype(BF16)
    for dt, ds in group:
        pt, ps = ahead(dt, ds)
        k = dt * n_s + ds
        go(remote(part, ranks.at[me], rk_send.at[k], rk_recv.at[k], {"tensor": pt, "sub": ps}))
    for c in range(PIECES):
        send_dy(c)
    for c in range(PIECES // 2, PIECES):
        forward(c)
    ranks[me] = part[...]

    following = infos[n_dp - 1, 0:1, :]
    goes_on = (following == customer[blocks - 1]) & (jnp.zeros_like(following) + d < n_dp - 1)
    limits[-1] = jnp.where(goes_on, BLOCK, limits[-1])
    limit = jnp.concatenate(limits, axis=1)
    lane = lax.broadcasted_iota(jnp.int32, (1, rows), 1)
    live = (jnp.bitwise_and(lane, BLOCK - 1) < limit).astype(F32)
    eye = lax.broadcasted_iota(jnp.int32, (BLOCK, BLOCK), 0) == lax.broadcasted_iota(
        jnp.int32, (BLOCK, BLOCK), 1)
    for b in range(blocks):
        at = slice(b * BLOCK, (b + 1) * BLOCK)
        column = jnp.sum(jnp.where(eye, live[:, at], 0.0), 1, keepdims=True)
        keep_rows[at, :] = jnp.broadcast_to(column, (BLOCK, BLOCK))

    def forward_far(c):
        for dt, ds in cross:
            ft, fs = behind(dt, ds)
            g = ft * n_s + fs
            k = dt * n_s + ds
            got_z = wfull.at[span(q_z, c), cols(g)]
            remote(got_z, got_z, wz_send.at[k, c], wz_recv.at[k, c], z_peer).wait_recv()
            got_y = wfull.at[span(q_y, c), cols(g)]
            remote(got_y, got_y, wy_send.at[k, c], wy_recv.at[k, c], y_peer).wait_recv()
            got, peer = (got_z, y_peer) if c < OVER_Y else (got_y, z_peer)
            go(remote(got, got, wd_send.at[k, c], wd_recv.at[k, c], peer))

    for c in range(PIECES // 2):
        forward_far(c)

    got = dyfull.at[:, cols(t * n_s + 1 - s)]
    remote(got, got, dc_send.at[0, 0], dc_recv.at[0, 0], core_peer).wait_recv()
    got = wfull.at[:, cols(t * n_s + 1 - s)]
    remote(got, got, wc_send, wc_recv, core_peer).wait_recv()

    @pl.loop(0, 4)
    def _(j):
        at = pl.ds(pl.multiple_of(j * quarter, quarter), quarter)
        acc[:, at] = dot_nt(dyfull[:, chip_cols(t)], wfull[at, chip_cols(t)])

    for dt, ds in group:
        ft, fs = behind(dt, ds)
        k = dt * n_s + ds
        remote(part, ranks.at[ft * n_s + fs], rk_send.at[k], rk_recv.at[k],
               {"tensor": ft, "sub": fs}).wait_recv()
    total = jnp.sum(ranks[...].astype(F32), 0)
    keep = drop * (SCALE * live)
    dropped = total[0:RANK] * keep
    grad_rank = total[RANK:2 * RANK] * keep
    dropped_all = jnp.where(own_slot, dropped[None], 0.0).reshape(n_dp * rk, rows).astype(BF16)
    grad_all = jnp.where(own_slot, grad_rank[None], 0.0).reshape(n_dp * rk, rows)
    up_part = dot_nn(dropped_all, dyfull[:, cols(me)])
    outgoing[:, :, width:] = up_part.reshape(n_dp, rk, vl).astype(BF16)
    down_part = dot_nn(grad_all.astype(BF16), x_ref[...])
    outgoing[:, :, :width] = down_part.reshape(n_dp, rk, width).astype(BF16)
    for off in range(1, n_dp):
        to = lax.rem(d + off, n_dp)
        go(remote(outgoing.at[to], incoming.at[off], out_send.at[off], out_recv.at[off], {"dp": to}))
    incoming[0] = outgoing[d]
    ranked[...] = grad_all.T.astype(BF16)

    for c in range(PIECES // 2, PIECES):
        forward_far(c)

    def pass_on(c):
        at = pl.ds(c * share, share)
        for dt in range(1, n_t):
            ft = lax.rem(t - dt + n_t, n_t)
            got = dyfull.at[at, cols(ft * n_s + s)]
            remote(got, got, dx_send.at[dt, c], dx_recv.at[dt, c], {"tensor": ft}).wait_recv()
            go(remote(got, got, dc_send.at[dt, c], dc_recv.at[dt, c], core_peer))
        for dt in range(1, n_t):
            got = dyfull.at[at, cols(lax.rem(t - dt + n_t, n_t) * n_s + 1 - s)]
            remote(got, got, dc_send.at[dt, c], dc_recv.at[dt, c], core_peer).wait_recv()

    @pl.loop(0, 4)
    def _(j):
        at = pl.ds(pl.multiple_of(j * quarter, quarter), quarter)
        acc[:, at] += dot_nn(ranked[...], downs[:, :, at].reshape(n_dp * rk, quarter))

    def finish(stage, q):
        first, end = STAGES[stage]
        high = pl.ds(first * share, (end - first) * share)
        at = pl.ds(pl.multiple_of(q * quarter, quarter), quarter)
        total = acc[high, at]
        for dt in range(1, n_t):
            far = chip_cols(lax.rem(t + dt, n_t))
            total += dot_nt(dyfull[high, far], wfull[at, far])
        live_row = jnp.concatenate([keep_rows[high, :]] * (quarter // BLOCK), axis=1)
        out_ref[high, at] = jnp.where(live_row > 0, total, 0.0).astype(BF16)

    def finish_all(stage):
        @pl.loop(0, 4)
        def _(q):
            finish(stage, q)

    for c in range(*STAGES[0]):
        pass_on(c)
    for q in (q_own, q_z, q_y):
        finish(0, q)

    for dt, ds in cross:
        ft, fs = behind(dt, ds)
        g = ft * n_s + fs
        k = dt * n_s + ds
        for c in range(PIECES):
            got = wfull.at[span(q_yz, c), cols(g)]
            remote(got, got, wd_send.at[k, c], wd_recv.at[k, c], y_peer if c < OVER_Y else z_peer).wait_recv()
    finish(0, q_yz)
    for stage in range(1, len(STAGES)):
        for c in range(*STAGES[stage]):
            pass_on(c)
        finish_all(stage)
    for off in range(1, n_dp):
        remote(outgoing.at[d], incoming.at[off], out_send.at[off], out_recv.at[off],
               {"dp": lax.rem(d - off + n_dp, n_dp)}).wait_recv()
    for j in range(local_slots):
        at = slice(j * RANK, (j + 1) * RANK)
        count = 0
        for tenant in range(tenants):
            count += jnp.where(slot_of[tenant] == d * local_slots + j, live_count[tenant], 0)
        sums = jnp.sum(incoming[:, at, :].astype(F32), 0)
        sums = sums / jnp.full((1, width + vl), count, jnp.int32).astype(F32)
        down_out[at, :] = sums[:, :width]
        up_out[at, :] = sums[:, width:]
    for copy in sent:
        copy.wait_send()


def body(x, dy, w, down_table, up_table, live_token_count, block_customer, customer_slot, dropout_flags):
    n_dp, n_t, n_s = (lax.axis_size(n) for n in ("dp", "tensor", "sub"))
    groups = n_t * n_s
    rows, width = x.shape
    vl = dy.shape[1]
    local_slots = down_table.shape[0]
    rk = local_slots * RANK
    all_rk = n_dp * rk
    vmem = pl.BlockSpec(memory_space=pltpu.VMEM)
    smem = pl.BlockSpec(memory_space=pltpu.SMEM)
    hbm = pl.BlockSpec(memory_space=pltpu.HBM)
    dma = pltpu.SemaphoreType.DMA
    input_grad, down_grad, up_grad = pl.pallas_call(
        functools.partial(kernel, (n_dp, n_t, n_s)),
        out_shape=(
            jax.ShapeDtypeStruct((rows, width), BF16),
            jax.ShapeDtypeStruct((rk, width), F32),
            jax.ShapeDtypeStruct((rk, vl), F32),
        ),
        in_specs=[hbm] * 5 + [smem] * 3 + [vmem],
        out_specs=(vmem, vmem, vmem),
        scratch_shapes=[
            pltpu.VMEM((rows, width), BF16),
            pltpu.VMEM((width, groups * vl), BF16),
            pltpu.VMEM((rows, groups * vl), BF16),
            pltpu.VMEM((rows, width), F32),
            pltpu.VMEM((n_dp, rk, width), BF16),
            pltpu.VMEM((n_dp, rk, vl), BF16),
            pltpu.VMEM((8, BLOCK), jnp.int32),
            pltpu.VMEM((n_dp, 8, BLOCK), jnp.int32),
            pltpu.VMEM((2 * RANK, rows), BF16),
            pltpu.VMEM((groups, 2 * RANK, rows), BF16),
            pltpu.VMEM((n_dp, rk, width + vl), BF16),
            pltpu.VMEM((n_dp, rk, width + vl), BF16),
            pltpu.VMEM((rows, BLOCK), F32),
            pltpu.VMEM((rows, all_rk), BF16),
            dma((5,)),
            dma((3, n_dp)), dma((3, n_dp)),
            dma((groups,)), dma((groups,)),
            dma((n_dp,)), dma((n_dp,)),
            dma((groups, PIECES)), dma((groups, PIECES)),
            dma((groups, PIECES)), dma((groups, PIECES)),
            dma((groups, PIECES)), dma((groups, PIECES)),
            dma((groups, PIECES)), dma((groups, PIECES)),
            dma, dma,
            dma((n_t, PIECES)), dma((n_t, PIECES)),
            dma((n_t, PIECES)), dma((n_t, PIECES)),
        ],
        compiler_params=pltpu.CompilerParams(
            collective_id=0, has_side_effects=True, vmem_limit_bytes=48 * 1024 * 1024
        ),
    )(x, stay(dy), w, stay(down_table.reshape(rk, width)), stay(up_table.reshape(rk, vl)),
      stay(live_token_count), stay(block_customer), stay(customer_slot), stay(dropout_flags.reshape(1, -1)))
    return input_grad, down_grad.reshape(local_slots, RANK, width), up_grad.reshape(local_slots, RANK, vl)


def solution(mesh):
    return jax.shard_map(
        body,
        mesh=mesh,
        in_specs=(
            P(("parts", "dp"), ("tensor", "sub")),
            P(("parts", "dp"), ("tensor", "sub")),
            P(None, ("tensor", "sub")),
            P(("parts", "dp"), None, ("tensor", "sub")),
            P(("parts", "dp"), None, ("tensor", "sub")),
            P("parts"),
            P(("parts", "dp")),
            P("parts"),
            P(("parts", "dp")),
        ),
        out_specs=(
            P(("parts", "dp"), ("tensor", "sub")),
            P(("parts", "dp"), None, ("tensor", "sub")),
            P(("parts", "dp"), None, ("tensor", "sub")),
        ),
        check_vma=False,
    )
```
